32 devices in a mesh: row: 8 (over y, x, core), cent: 4 (over z).
Axes of the slice: x: 2, y: 2, z: 4, core: 2. Of those that a mesh axis runs over, the one named last changes fastest.
Arguments:
- embeddings: bfloat16 [4096, 1536], P('row'), may hold values from -48 to 48
- centroids: bfloat16 [1024, 1536], P('cent'), may hold values from -0.5 to 0.5
Outputs:
- centroids_out: bfloat16 [1024, 1536], P('cent')
- energy: float32 [4096], P('row')
The draws below stay inside these ranges and needn't reach their ends.
All inputs are finite; a program needn't handle non-finite values.
Results may differ from the reference program's by a relative error of at most 0.0091.
Values may be sent and summed in bfloat16 or wider, within the bound.
A program may use at most 64 MiB of HBM per device.

```python
import math
import jax
import jax.numpy as jnp
from jax import lax

D = 1536
ITERS = 2
ROWS = 4096
K = 1024


def base_centroids(key):
    limit = min(6.0, math.sqrt(D) / 6.0)
    return jax.random.truncated_normal(key, -limit, limit, (K, D), jnp.float32) * (3.0 / math.sqrt(D))


def draw_centroids(key, part):
    shared = base_centroids(key)
    return shared.astype(jnp.bfloat16)


def draw_embeddings(key, part):
    key = jax.random.fold_in(key, 9)
    positions = jnp.arange(ROWS, dtype=jnp.float32)[:, None]
    ramp = 0.6 + 1.2 * positions / max(ROWS - 1, 1)
    return (ramp * jax.random.truncated_normal(key, -6.0, 6.0, (ROWS, D), jnp.float32)).astype(jnp.bfloat16)


def setup_inputs(seed: int = 0) -> dict:
    streams_of = jax.random.split(jax.random.key(seed), 3)
    embeddings = draw_embeddings(jax.random.fold_in(streams_of[2], 71), 0)
    centroids = draw_centroids(jax.random.fold_in(streams_of[2], 71), 0)
    return dict(embeddings=embeddings, centroids=centroids)


PRIOR_WEIGHT = 8.0


def one_pass(embeddings, current):
    block_rows = math.gcd(ROWS, 4096)
    squared = jnp.sum(jnp.square(current.astype(jnp.float32)), axis=1)
    blocks = embeddings.reshape(ROWS // block_rows, block_rows, D)

    def advance(carry, block_x):
        totals, mass = carry
        scores = jnp.dot(block_x, current.T, preferred_element_type=jnp.float32) - 0.5 * squared[None, :]
        row_top = jnp.max(scores, axis=1)
        lifted = jnp.exp(scores - row_top[:, None])
        row_total = jnp.sum(lifted, axis=1)
        weights = (lifted / row_total[:, None]).astype(jnp.bfloat16)
        totals = totals + jnp.dot(weights.T, block_x, preferred_element_type=jnp.float32)
        mass = mass + jnp.sum(weights.astype(jnp.float32), axis=0)
        return (totals, mass), row_top + jnp.log(row_total)

    start = (jnp.zeros((K, D), jnp.float32), jnp.zeros((K,), jnp.float32))
    (totals, mass), energy = lax.scan(advance, start, blocks)
    updated = (totals + PRIOR_WEIGHT * current.astype(jnp.float32)) / (mass + PRIOR_WEIGHT)[:, None]
    return updated.astype(jnp.bfloat16), energy.reshape(ROWS)


def reference(embeddings, centroids):
    current = centroids
    energy = jnp.zeros((ROWS,), jnp.float32)
    for iteration in range(ITERS):
        current, found = one_pass(embeddings, current)
        if iteration == 0:
            energy = found
    return current, energy
```

```python
import functools

import jax
import jax.numpy as jnp
from jax import lax
from jax.experimental import pallas as pl
from jax.experimental.pallas import tpu as pltpu
from jax.sharding import PartitionSpec as P

ITERS = 2
PRIOR_WEIGHT = 8.0
CHUNKS = 2
MESH = pl.DeviceIdType.MESH
NT = (((1,), (1,)), ((), ()))


def score_against(embeddings, cluster_block):
    squared = jnp.sum(jnp.square(cluster_block.astype(jnp.float32)), axis=1)
    inner = lax.dot_general(embeddings, cluster_block, NT, preferred_element_type=jnp.float32)
    return inner - 0.5 * squared[None, :]


def updated_rows(totals, mass, previous):
    blended = (totals + PRIOR_WEIGHT * previous.astype(jnp.float32)) / (mass + PRIOR_WEIGHT)[
        :, None
    ]
    return blended.astype(jnp.bfloat16)


def local_plain(embeddings, centroids):
    row_count = embeddings.shape[0]
    cluster_count = centroids.shape[0]
    share_rows = cluster_count // lax.axis_size("row")
    shares = lax.dynamic_slice_in_dim(centroids, lax.axis_index("row") * share_rows, share_rows, 0)
    energy = jnp.zeros((row_count,), jnp.float32)
    for iteration in range(ITERS):
        if iteration == 0:
            scores = score_against(embeddings, centroids)
        else:
            scores = score_against(embeddings, lax.all_gather(shares, "row", axis=0, tiled=True))
        row_top = lax.pmax(jnp.max(scores, axis=1), "cent")
        lifted = jnp.exp(scores - row_top[:, None])
        row_total = lax.psum(jnp.sum(lifted, axis=1), "cent")
        weights = (lifted / row_total[:, None]).astype(jnp.bfloat16)
        totals = lax.dot_general(
            weights, embeddings, (((0,), (0,)), ((), ())), preferred_element_type=jnp.float32
        )
        mass = jnp.sum(weights.astype(jnp.float32), axis=0)
        energies = row_top + jnp.log(row_total)
        if iteration == 0:
            energy = energies
        share_totals, share_mass = (
            lax.psum_scatter(totals, "row", scatter_dimension=0, tiled=True),
            lax.psum_scatter(mass, "row", scatter_dimension=0, tiled=True),
        )
        shares = updated_rows(share_totals, share_mass, shares)
    result = lax.all_gather(shares, "row", axis=0, tiled=True)
    return (result, energy)


def kernel(
    groups, chunks,
    x_hbm, c_hbm, out_hbm, energy_ref,
    xs, cs, wt, st, sq, mass_col,
    stat_send, stat_recv, mass_send, mass_recv,
    s0, r0, k0, s1, r1, k1, s2, r2, k2, cc,
    load_sem, out_sem, stat_ss, stat_rs, mass_ss, mass_rs, ring_ss, ring_rs,
):
    rows, depth = xs.shape
    count = cs.shape[0]
    width = depth // chunks
    half, quarter, eighth = count // 2, count // 4, count // 8
    r = lax.axis_index("row")
    z = lax.axis_index("cent")
    core = lax.rem(r, 2)
    px = lax.rem(r // 2, 2)
    py = r // 4
    sibling = r + 1 - 2 * core
    flip_x = 2 * (1 - 2 * px)
    flip_y = 4 * (1 - 2 * py)
    first = r + (1 - core) * flip_x + core * flip_y
    second = r + core * flip_x + (1 - core) * flip_y
    a = (1 - core) * px + core * py
    b = (1 - core) * py + core * px
    base_half = pl.multiple_of(core * half, half)
    other_half = pl.multiple_of((1 - core) * half, half)
    base_quarter = pl.multiple_of(core * half + a * quarter, quarter)
    base = pl.multiple_of(core * half + a * quarter + b * eighth, eighth)
    mine_q = pl.multiple_of(a * quarter, quarter)
    theirs_q = pl.multiple_of((1 - a) * quarter, quarter)
    mine_e = pl.multiple_of(b * eighth, eighth)
    theirs_e = pl.multiple_of((1 - b) * eighth, eighth)

    barrier = pltpu.get_barrier_semaphore()
    for d in range(1, 8):
        pl.semaphore_signal(
            barrier, inc=1, device_id=(lax.rem(r + d, 8), z), device_id_type=MESH
        )
    for d in range(1, groups):
        pl.semaphore_signal(
            barrier, inc=1, device_id=(r, lax.rem(z + d, groups)), device_id_type=MESH
        )
    loads = [
        pltpu.make_async_copy(c_hbm, cs, load_sem.at[0]),
        pltpu.make_async_copy(x_hbm, xs, load_sem.at[1]),
    ]
    for load in loads:
        load.start()

    sends = []

    def remote(src, dst, ss, rs, device):
        copy = pltpu.make_async_remote_copy(
            src_ref=src, dst_ref=dst, send_sem=ss, recv_sem=rs,
            device_id=device, device_id_type=MESH,
        )
        copy.start()
        sends.append(copy)
        return copy

    def cols(j):
        return pl.ds(j * width, width)

    def norms(block):
        wide = block.astype(jnp.float32)
        return jnp.sum(wide * wide, axis=1, keepdims=True)

    for load in loads:
        load.wait()
    st[...] = lax.dot_general(cs[...], xs[...], NT, preferred_element_type=jnp.float32)
    sq[...] = norms(cs[...])

    for it in range(ITERS):
        shifted = st[...] - 0.5 * sq[...]
        top = jnp.max(shifted, axis=0, keepdims=True)
        lifted = jnp.exp(shifted - top)
        total = jnp.sum(lifted, axis=0, keepdims=True)
        stat_send[it, 0:1, :] = top
        stat_send[it, 1:2, :] = total
        if it == 0:
            pl.semaphore_wait(barrier, 7 + groups - 1)
        arrivals = []
        for d in range(1, groups):
            arrivals.append(
                remote(
                    stat_send.at[it], stat_recv.at[it, d - 1],
                    stat_ss.at[it, d - 1], stat_rs.at[it, d - 1],
                    (r, lax.rem(z + d, groups)),
                )
            )
        st[...] = lifted
        all_top, tops, sums = top, [top], [total]
        for d in range(1, groups):
            arrivals[d - 1].wait_recv()
            tops.append(stat_recv[it, d - 1, 0:1, :])
            sums.append(stat_recv[it, d - 1, 1:2, :])
            all_top = jnp.maximum(all_top, tops[-1])
        all_total = jnp.zeros_like(total)
        for t, s in zip(tops, sums):
            all_total = all_total + s * jnp.exp(t - all_top)
        if it == 0:
            energy_ref[...] = all_top + jnp.log(all_total)
        scale = jnp.exp(top - all_top) / all_total
        weights = (st[...] * scale).astype(jnp.bfloat16)
        wt[...] = weights

        mass_send[it] = lax.dot_general(
            jnp.ones((8, rows), jnp.bfloat16), weights, NT, preferred_element_type=jnp.float32
        )
        masses = []

        def send_masses(it=it, masses=masses):
            for d in range(1, 8):
                masses.append(
                    remote(
                        mass_send.at[it], mass_recv.at[it, d - 1],
                        mass_ss.at[it, d - 1], mass_rs.at[it, d - 1],
                        (lax.rem(r + d, 8), z),
                    )
                )

        flights = {}

        def stage0(j, it=it):
            part = jnp.dot(
                wt[pl.ds(other_half, half), :], xs[:, cols(j)], preferred_element_type=jnp.float32
            )
            s0[it, j] = part.astype(jnp.bfloat16)
            flights[0, j] = remote(
                s0.at[it, j], r0.at[it, j], ring_ss.at[it, j, 0], ring_rs.at[it, j, 0], (sibling, z)
            )
            if j == 0:
                send_masses()
            k0[j] = jnp.dot(
                wt[pl.ds(base_half, half), :], xs[:, cols(j)], preferred_element_type=jnp.float32
            )

        def stage1(j, it=it):
            flights[0, j].wait_recv()
            there, here = pl.ds(theirs_q, quarter), pl.ds(mine_q, quarter)
            s1[it, j] = (k0[j, there] + r0[it, j, there].astype(jnp.float32)).astype(jnp.bfloat16)
            flights[1, j] = remote(
                s1.at[it, j], r1.at[it, j], ring_ss.at[it, j, 1], ring_rs.at[it, j, 1], (first, z)
            )
            k1[j] = k0[j, here] + r0[it, j, here].astype(jnp.float32)

        def stage2(j, it=it):
            flights[1, j].wait_recv()
            there, here = pl.ds(theirs_e, eighth), pl.ds(mine_e, eighth)
            s2[it, j] = (k1[j, there] + r1[it, j, there].astype(jnp.float32)).astype(jnp.bfloat16)
            flights[2, j] = remote(
                s2.at[it, j], r2.at[it, j], ring_ss.at[it, j, 2], ring_rs.at[it, j, 2], (second, z)
            )
            k2[j] = k1[j, here] + r1[it, j, here].astype(jnp.float32)
            if j == 0:
                everyone = mass_send[it]
                for d in range(1, 8):
                    masses[d - 1].wait_recv()
                    everyone = everyone + mass_recv[it, d - 1]
                tall = jnp.concatenate([everyone] * 16, axis=0)
                mass_col[...] = 1.0 / (jnp.transpose(tall) + PRIOR_WEIGHT)

        def stage3(j, it=it):
            flights[2, j].wait_recv()
            mine = pl.ds(base, eighth)
            old = cs[mine, cols(j)] if it == 0 else cc[it - 1, j, mine]
            sums = k2[j] + r2[it, j].astype(jnp.float32) + PRIOR_WEIGHT * old.astype(jnp.float32)
            cc[it, j, mine] = (sums * mass_col[mine, 0:1]).astype(jnp.bfloat16)
            place = cc.at[it, j, mine]
            flights[3, j] = remote(
                place, place, ring_ss.at[it, j, 3], ring_rs.at[it, j, 3], (second, z)
            )

        def stage4(j, it=it):
            flights[3, j].wait_recv()
            place = cc.at[it, j, pl.ds(base_quarter, quarter)]
            flights[4, j] = remote(
                place, place, ring_ss.at[it, j, 4], ring_rs.at[it, j, 4], (first, z)
            )

        def stage5(j, it=it):
            flights[4, j].wait_recv()
            place = cc.at[it, j, pl.ds(base_half, half)]
            flights[5, j] = remote(
                place, place, ring_ss.at[it, j, 5], ring_rs.at[it, j, 5], (sibling, z)
            )

        def stage6(j, it=it):
            flights[5, j].wait_recv()
            if it == ITERS - 1:
                copy = pltpu.make_async_copy(cc.at[it, j], out_hbm.at[:, cols(j)], out_sem.at[j])
                copy.start()
                outs.append(copy)
                return
            block = cc[it, j]
            inner = lax.dot_general(block, xs[:, cols(j)], NT, preferred_element_type=jnp.float32)
            if j == 0:
                st[...] = inner
                sq[...] = norms(block)
            else:
                st[...] += inner
                sq[...] += norms(block)

        outs = []
        stages = [stage0, stage1, stage2, stage3, stage4, stage5, stage6]
        for tick in range(chunks + len(stages) - 1):
            for s in reversed(range(len(stages))):
                if 0 <= tick - s < chunks:
                    stages[s](tick - s)
        for copy in outs:
            copy.wait()

    for copy in sends:
        copy.wait_send()


def local_fused(groups, embeddings, centroids):
    rows, depth = embeddings.shape
    count = centroids.shape[0]
    chunks = CHUNKS
    width = depth // chunks
    half, quarter, eighth = count // 2, count // 4, count // 8
    bf16, f32 = jnp.bfloat16, jnp.float32
    dma = pltpu.SemaphoreType.DMA
    result, energy = pl.pallas_call(
        functools.partial(kernel, groups, chunks),
        out_shape=(
            jax.ShapeDtypeStruct((count, depth), bf16),
            jax.ShapeDtypeStruct((1, rows), f32),
        ),
        in_specs=[pl.BlockSpec(memory_space=pl.ANY)] * 2,
        out_specs=(
            pl.BlockSpec(memory_space=pl.ANY),
            pl.BlockSpec(memory_space=pltpu.VMEM),
        ),
        scratch_shapes=[
            pltpu.VMEM((rows, depth), bf16),
            pltpu.VMEM((count, depth), bf16),
            pltpu.VMEM((count, rows), bf16),
            pltpu.VMEM((count, rows), f32),
            pltpu.VMEM((count, 1), f32),
            pltpu.VMEM((count, 128), f32),
            pltpu.VMEM((ITERS, 2, rows), f32),
            pltpu.VMEM((ITERS, groups - 1, 2, rows), f32),
            pltpu.VMEM((ITERS, 8, count), f32),
            pltpu.VMEM((ITERS, 7, 8, count), f32),
            pltpu.VMEM((ITERS, chunks, half, width), bf16),
            pltpu.VMEM((ITERS, chunks, half, width), bf16),
            pltpu.VMEM((chunks, half, width), f32),
            pltpu.VMEM((ITERS, chunks, quarter, width), bf16),
            pltpu.VMEM((ITERS, chunks, quarter, width), bf16),
            pltpu.VMEM((chunks, quarter, width), f32),
            pltpu.VMEM((ITERS, chunks, eighth, width), bf16),
            pltpu.VMEM((ITERS, chunks, eighth, width), bf16),
            pltpu.VMEM((chunks, eighth, width), f32),
            pltpu.VMEM((ITERS, chunks, count, width), bf16),
            dma((2,)),
            dma((chunks,)),
            dma((ITERS, groups - 1)),
            dma((ITERS, groups - 1)),
            dma((ITERS, 7)),
            dma((ITERS, 7)),
            dma((ITERS, chunks, 6)),
            dma((ITERS, chunks, 6)),
        ],
        compiler_params=pltpu.CompilerParams(
            collective_id=0, has_side_effects=True, vmem_limit_bytes=48 * 1024 * 1024
        ),
        cost_estimate=pl.CostEstimate(
            flops=8 * rows * count * depth,
            bytes_accessed=2 * depth * (rows + 2 * count),
            transcendentals=2 * rows * count,
        ),
    )(embeddings, centroids)
    return result, energy.reshape(rows)


def solution(mesh):
    def local(embeddings, centroids):
        rows, depth = embeddings.shape
        count = centroids.shape[0]
        groups = mesh.shape["cent"]
        fits = (
            mesh.shape["row"] == 8
            and groups > 1
            and rows % 256 == 0
            and rows <= 1024
            and count == 256
            and depth % (128 * CHUNKS) == 0
        )
        if fits:
            return local_fused(groups, embeddings, centroids)
        return local_plain(embeddings, centroids)

    return jax.shard_map(
        local,
        mesh=mesh,
        in_specs=(P("row", None), P("cent", None)),
        out_specs=(P("cent", None), P("row")),
        check_vma=False,
    )
```

```python
import functools

import jax
import jax.numpy as jnp
from jax import lax
from jax.experimental import pallas as pl
from jax.experimental.pallas import tpu as pltpu
from jax.sharding import PartitionSpec as P

ITERS = 2
PRIOR_WEIGHT = 8.0
CHUNKS = 2
MESH = pl.DeviceIdType.MESH
NT = (((1,), (1,)), ((), ()))


def score_against(embeddings, cluster_block):
    squared = jnp.sum(jnp.square(cluster_block.astype(jnp.float32)), axis=1)
    inner = lax.dot_general(embeddings, cluster_block, NT, preferred_element_type=jnp.float32)
    return inner - 0.5 * squared[None, :]


def updated_rows(totals, mass, previous):
    blended = (totals + PRIOR_WEIGHT * previous.astype(jnp.float32)) / (mass + PRIOR_WEIGHT)[
        :, None
    ]
    return blended.astype(jnp.bfloat16)


def local_plain(embeddings, centroids):
    row_count = embeddings.shape[0]
    cluster_count = centroids.shape[0]
    share_rows = cluster_count // lax.axis_size("row")
    shares = lax.dynamic_slice_in_dim(centroids, lax.axis_index("row") * share_rows, share_rows, 0)
    energy = jnp.zeros((row_count,), jnp.float32)
    for iteration in range(ITERS):
        if iteration == 0:
            scores = score_against(embeddings, centroids)
        else:
            scores = score_against(embeddings, lax.all_gather(shares, "row", axis=0, tiled=True))
        row_top = lax.pmax(jnp.max(scores, axis=1), "cent")
        lifted = jnp.exp(scores - row_top[:, None])
        row_total = lax.psum(jnp.sum(lifted, axis=1), "cent")
        weights = (lifted / row_total[:, None]).astype(jnp.bfloat16)
        totals = lax.dot_general(
            weights, embeddings, (((0,), (0,)), ((), ())), preferred_element_type=jnp.float32
        )
        mass = jnp.sum(weights.astype(jnp.float32), axis=0)
        energies = row_top + jnp.log(row_total)
        if iteration == 0:
            energy = energies
        share_totals, share_mass = (
            lax.psum_scatter(totals, "row", scatter_dimension=0, tiled=True),
            lax.psum_scatter(mass, "row", scatter_dimension=0, tiled=True),
        )
        shares = updated_rows(share_totals, share_mass, shares)
    result = lax.all_gather(shares, "row", axis=0, tiled=True)
    return (result, energy)


def kernel(
    groups, chunks,
    x_hbm, c_hbm, out_hbm, energy_ref,
    xs, cs, wt, st, sq, mass_col,
    stat_send, stat_recv, mass_send, mass_recv,
    s0, r0, k0, s1, r1, cc,
    load_sem, out_sem, stat_ss, stat_rs, mass_ss, mass_rs, ring_ss, ring_rs,
):
    rows, depth = xs.shape
    count = cs.shape[0]
    width = depth // chunks
    half, share = count // 2, count // 8
    r = lax.axis_index("row")
    z = lax.axis_index("cent")
    core = lax.rem(r, 2)
    px = lax.rem(r // 2, 2)
    py = r // 4
    sibling = r + 1 - 2 * core
    flips = (1 - 2 * px, 2 * (1 - 2 * py), 1 - 2 * px + 2 * (1 - 2 * py))
    chip = r // 2
    base_half = pl.multiple_of(core * half, half)
    other_half = pl.multiple_of((1 - core) * half, half)

    def part(owner):
        return pl.ds(pl.multiple_of(owner * share, share), share)

    def place(core_of, owner):
        return pl.ds(pl.multiple_of(core_of * half + owner * share, share), share)

    barrier = pltpu.get_barrier_semaphore()
    for d in range(1, groups):
        pl.semaphore_signal(
            barrier, inc=1, device_id=(r, lax.rem(z + d, groups)), device_id_type=MESH
        )
    for d in range(1, 8):
        pl.semaphore_signal(
            barrier, inc=1, device_id=(lax.rem(r + d, 8), z), device_id_type=MESH
        )
    loads = [
        pltpu.make_async_copy(c_hbm, cs, load_sem.at[0]),
        pltpu.make_async_copy(x_hbm, xs, load_sem.at[1]),
    ]
    for load in loads:
        load.start()

    sends = []

    def remote(src, dst, ss, rs, device):
        copy = pltpu.make_async_remote_copy(
            src_ref=src, dst_ref=dst, send_sem=ss, recv_sem=rs,
            device_id=device, device_id_type=MESH,
        )
        copy.start()
        sends.append(copy)
        return copy

    def cols(j):
        return pl.ds(j * width, width)

    def norms(block):
        wide = block.astype(jnp.float32)
        return jnp.sum(wide * wide, axis=1, keepdims=True)

    for load in loads:
        load.wait()
    st[...] = lax.dot_general(cs[...], xs[...], NT, preferred_element_type=jnp.float32)
    sq[...] = norms(cs[...])

    for it in range(ITERS):
        shifted = st[...] - 0.5 * sq[...]
        top = jnp.max(shifted, axis=0, keepdims=True)
        lifted = jnp.exp(shifted - top)
        total = jnp.sum(lifted, axis=0, keepdims=True)
        stat_send[it, 0:1, :] = top
        stat_send[it, 1:2, :] = total
        if it == 0:
            pl.semaphore_wait(barrier, 7 + groups - 1)
        arrivals = []
        for d in range(1, groups):
            arrivals.append(
                remote(
                    stat_send.at[it], stat_recv.at[it, d - 1],
                    stat_ss.at[it, d - 1], stat_rs.at[it, d - 1],
                    (r, lax.rem(z + d, groups)),
                )
            )
        st[...] = lifted
        all_top, tops, sums = top, [top], [total]
        for d in range(1, groups):
            arrivals[d - 1].wait_recv()
            tops.append(stat_recv[it, d - 1, 0:1, :])
            sums.append(stat_recv[it, d - 1, 1:2, :])
            all_top = jnp.maximum(all_top, tops[-1])
        all_total = jnp.zeros_like(total)
        for t, s in zip(tops, sums):
            all_total = all_total + s * jnp.exp(t - all_top)
        if it == 0:
            energy_ref[...] = all_top + jnp.log(all_total)
        scale = jnp.exp(top - all_top) / all_total
        wt[...] = (st[...] * scale).astype(jnp.bfloat16)

        masses = []
        flights = {}
        outs = []

        def sums0(j, it=it):
            piece = jnp.dot(
                wt[pl.ds(other_half, half), :], xs[:, cols(j)], preferred_element_type=jnp.float32
            )
            s0[it, j] = piece.astype(jnp.bfloat16)
            flights[0, j] = remote(
                s0.at[it, j], r0.at[it, j], ring_ss.at[it, j, 0], ring_rs.at[it, j, 0], (sibling, z)
            )
            k0[j] = jnp.dot(
                wt[pl.ds(base_half, half), :], xs[:, cols(j)], preferred_element_type=jnp.float32
            )

        def send_masses(it=it):
            mass_send[it] = lax.dot_general(
                jnp.ones((8, rows), jnp.bfloat16), wt[...], NT, preferred_element_type=jnp.float32
            )[0:1, :]
            for d in range(1, 8):
                masses.append(
                    remote(
                        mass_send.at[it], mass_recv.at[it, d - 1],
                        mass_ss.at[it, d - 1], mass_rs.at[it, d - 1],
                        (lax.rem(r + d, 8), z),
                    )
                )

        def sums1(j, it=it):
            flights[0, j].wait_recv()
            both = k0[j] + r0[it, j].astype(jnp.float32)
            k0[j] = both
            s1[it, j] = both.astype(jnp.bfloat16)
            for p in (2, 0, 1):
                flights[1 + p, j] = remote(
                    s1.at[it, j, part(chip + flips[p])], r1.at[it, j, p],
                    ring_ss.at[it, j, 1 + p], ring_rs.at[it, j, 1 + p],
                    (r + 2 * flips[p], z),
                )

        def take_masses(it=it):
            everyone = mass_send[it]
            for d in range(1, 8):
                masses[d - 1].wait_recv()
                everyone = everyone + mass_recv[it, d - 1]
            tall = jnp.broadcast_to(everyone, (128, count))
            mass_col[...] = 1.0 / (jnp.transpose(tall) + PRIOR_WEIGHT)

        def update(j, it=it):
            mine = place(core, chip)
            old = cs[mine, cols(j)] if it == 0 else cc[it - 1, j, mine]
            blend = k0[j, part(chip)] + PRIOR_WEIGHT * old.astype(jnp.float32)
            for p in range(3):
                flights[1 + p, j].wait_recv()
                blend = blend + r1[it, j, p].astype(jnp.float32)
            cc[it, j, mine] = (blend * mass_col[mine, 0:1]).astype(jnp.bfloat16)
            here = cc.at[it, j, mine]
            for p in (2, 0, 1):
                flights[4 + p, j] = remote(
                    here, here, ring_ss.at[it, j, 4 + p], ring_rs.at[it, j, 4 + p],
                    (r + 2 * flips[p], z),
                )
            save(j, 0, mine)
            flights[7, j] = remote(
                here, here, ring_ss.at[it, j, 7], ring_rs.at[it, j, 7], (sibling, z)
            )

        def save(j, n, rows_of, it=it):
            if it == ITERS - 1:
                copy = pltpu.make_async_copy(
                    cc.at[it, j, rows_of], out_hbm.at[rows_of, cols(j)], out_sem.at[j, n]
                )
                copy.start()
                outs.append(copy)

        def forward(j, it=it):
            for p in range(3):
                flights[4 + p, j].wait_recv()
                here = cc.at[it, j, place(core, chip + flips[p])]
                flights[8 + p, j] = remote(
                    here, here, ring_ss.at[it, j, 8 + p], ring_rs.at[it, j, 8 + p], (sibling, z)
                )
                save(j, 1 + p, place(core, chip + flips[p]))

        def use(j, it=it):
            for p, flip in enumerate((0,) + flips):
                flights[7 + p, j].wait_recv()
                save(j, 4 + p, place(1 - core, chip + flip))
            if it == ITERS - 1:
                return
            block = cc[it, j]
            inner = lax.dot_general(block, xs[:, cols(j)], NT, preferred_element_type=jnp.float32)
            if j == 0:
                st[...] = inner
                sq[...] = norms(block)
            else:
                st[...] += inner
                sq[...] += norms(block)

        for j in range(chunks):
            sums0(j)
        send_masses()
        for j in range(chunks):
            sums1(j)
        take_masses()
        for j in range(chunks):
            update(j)
        for j in range(chunks):
            forward(j)
        for j in range(chunks):
            use(j)
        for copy in outs:
            copy.wait()

    for copy in sends:
        copy.wait_send()


def local_fused(groups, embeddings, centroids):
    rows, depth = embeddings.shape
    count = centroids.shape[0]
    chunks = CHUNKS
    width = depth // chunks
    half, share = count // 2, count // 8
    bf16, f32 = jnp.bfloat16, jnp.float32
    dma = pltpu.SemaphoreType.DMA
    result, energy = pl.pallas_call(
        functools.partial(kernel, groups, chunks),
        out_shape=(
            jax.ShapeDtypeStruct((count, depth), bf16),
            jax.ShapeDtypeStruct((1, rows), f32),
        ),
        in_specs=[pl.BlockSpec(memory_space=pl.ANY)] * 2,
        out_specs=(
            pl.BlockSpec(memory_space=pl.ANY),
            pl.BlockSpec(memory_space=pltpu.VMEM),
        ),
        scratch_shapes=[
            pltpu.VMEM((rows, depth), bf16),
            pltpu.VMEM((count, depth), bf16),
            pltpu.VMEM((count, rows), bf16),
            pltpu.VMEM((count, rows), f32),
            pltpu.VMEM((count, 1), f32),
            pltpu.VMEM((count, 128), f32),
            pltpu.VMEM((ITERS, 2, rows), f32),
            pltpu.VMEM((ITERS, groups - 1, 2, rows), f32),
            pltpu.VMEM((ITERS, 1, count), f32),
            pltpu.VMEM((ITERS, 7, 1, count), f32),
            pltpu.VMEM((ITERS, chunks, half, width), bf16),
            pltpu.VMEM((ITERS, chunks, half, width), bf16),
            pltpu.VMEM((chunks, half, width), f32),
            pltpu.VMEM((ITERS, chunks, half, width), bf16),
            pltpu.VMEM((ITERS, chunks, 3, share, width), bf16),
            pltpu.VMEM((ITERS, chunks, count, width), bf16),
            dma((2,)),
            dma((chunks, 8)),
            dma((ITERS, groups - 1)),
            dma((ITERS, groups - 1)),
            dma((ITERS, 7)),
            dma((ITERS, 7)),
            dma((ITERS, chunks, 11)),
            dma((ITERS, chunks, 11)),
        ],
        compiler_params=pltpu.CompilerParams(
            collective_id=0, has_side_effects=True, vmem_limit_bytes=63 * 1024 * 1024
        ),
        cost_estimate=pl.CostEstimate(
            flops=8 * rows * count * depth,
            bytes_accessed=2 * depth * (rows + 2 * count),
            transcendentals=2 * rows * count,
        ),
    )(embeddings, centroids)
    return result, energy.reshape(rows)


def solution(mesh):
    def local(embeddings, centroids):
        rows, depth = embeddings.shape
        count = centroids.shape[0]
        groups = mesh.shape["cent"]
        fits = (
            mesh.shape["row"] == 8
            and groups > 1
            and rows % 256 == 0
            and rows <= 1024
            and count == 256
            and depth % (128 * CHUNKS) == 0
        )
        if fits:
            return local_fused(groups, embeddings, centroids)
        return local_plain(embeddings, centroids)

    return jax.shard_map(
        local,
        mesh=mesh,
        in_specs=(P("row", None), P("cent", None)),
        out_specs=(P("cent", None), P("row")),
        check_vma=False,
    )
```

```python
import functools

import jax
import jax.numpy as jnp
from jax import lax
from jax.experimental import pallas as pl
from jax.experimental.pallas import tpu as pltpu
from jax.sharding import PartitionSpec as P

ITERS = 2
PRIOR_WEIGHT = 8.0
CHUNKS = 2
MESH = pl.DeviceIdType.MESH
NT = (((1,), (1,)), ((), ()))


def score_against(embeddings, cluster_block):
    squared = jnp.sum(jnp.square(cluster_block.astype(jnp.float32)), axis=1)
    inner = lax.dot_general(embeddings, cluster_block, NT, preferred_element_type=jnp.float32)
    return inner - 0.5 * squared[None, :]


def updated_rows(totals, mass, previous):
    blended = (totals + PRIOR_WEIGHT * previous.astype(jnp.float32)) / (mass + PRIOR_WEIGHT)[
        :, None
    ]
    return blended.astype(jnp.bfloat16)


def local_plain(embeddings, centroids):
    row_count = embeddings.shape[0]
    cluster_count = centroids.shape[0]
    share_rows = cluster_count // lax.axis_size("row")
    shares = lax.dynamic_slice_in_dim(centroids, lax.axis_index("row") * share_rows, share_rows, 0)
    energy = jnp.zeros((row_count,), jnp.float32)
    for iteration in range(ITERS):
        if iteration == 0:
            scores = score_against(embeddings, centroids)
        else:
            scores = score_against(embeddings, lax.all_gather(shares, "row", axis=0, tiled=True))
        row_top = lax.pmax(jnp.max(scores, axis=1), "cent")
        lifted = jnp.exp(scores - row_top[:, None])
        row_total = lax.psum(jnp.sum(lifted, axis=1), "cent")
        weights = (lifted / row_total[:, None]).astype(jnp.bfloat16)
        totals = lax.dot_general(
            weights, embeddings, (((0,), (0,)), ((), ())), preferred_element_type=jnp.float32
        )
        mass = jnp.sum(weights.astype(jnp.float32), axis=0)
        energies = row_top + jnp.log(row_total)
        if iteration == 0:
            energy = energies
        share_totals, share_mass = (
            lax.psum_scatter(totals, "row", scatter_dimension=0, tiled=True),
            lax.psum_scatter(mass, "row", scatter_dimension=0, tiled=True),
        )
        shares = updated_rows(share_totals, share_mass, shares)
    result = lax.all_gather(shares, "row", axis=0, tiled=True)
    return (result, energy)


def kernel(
    groups, chunks,
    x_hbm, c_hbm, out_hbm, energy_ref,
    xs, cs, wt, st1, er, st2, sq, mass_col,
    stat_send1, stat_recv1, stat_send2, stat_recv2, mass_send, mass_recv,
    k0, s1, r1, cc,
    load_sem, out_sem, x_ss, x_rs, e_ss, e_rs, stat_ss, stat_rs, mass_ss, mass_rs,
    ring_ss, ring_rs,
):
    rows, depth = x_hbm.shape
    count = cs.shape[0]
    width = depth // chunks
    half, share = count // 2, count // 8
    r = lax.axis_index("row")
    z = lax.axis_index("cent")
    core = lax.rem(r, 2)
    px = lax.rem(r // 2, 2)
    py = r // 4
    sibling = r + 1 - 2 * core
    flips = (1 - 2 * px, 2 * (1 - 2 * py), 1 - 2 * px + 2 * (1 - 2 * py))
    chip = r // 2
    my_half = pl.ds(pl.multiple_of(core * half, half), half)
    other_half = pl.ds(pl.multiple_of((1 - core) * half, half), half)
    my_rows = pl.ds(pl.multiple_of(core * rows, rows), rows)
    other_rows = pl.ds(pl.multiple_of((1 - core) * rows, rows), rows)

    def part(owner):
        return pl.ds(pl.multiple_of(owner * share, share), share)

    def place(core_of, owner):
        return pl.ds(pl.multiple_of(core_of * half + owner * share, share), share)

    column = [
        (2 * d + flip - 1, flip, (r + flip * (1 - 2 * core), lax.rem(z + d, groups)))
        for d in range(groups)
        for flip in range(2)
        if d + flip > 0
    ]
    column = sorted(column, key=lambda entry: -entry[0])

    barrier = pltpu.get_barrier_semaphore()
    for _, _, device in column:
        pl.semaphore_signal(barrier, inc=1, device_id=device, device_id_type=MESH)
    for p in range(3):
        pl.semaphore_signal(
            barrier, inc=1, device_id=(r + 2 * flips[p], z), device_id_type=MESH
        )
    loads = [
        pltpu.make_async_copy(x_hbm, xs.at[my_rows], load_sem.at[0]),
        pltpu.make_async_copy(c_hbm, cs, load_sem.at[1]),
    ]
    for load in loads:
        load.start()

    sends = []

    def remote(src, dst, ss, rs, device):
        copy = pltpu.make_async_remote_copy(
            src_ref=src, dst_ref=dst, send_sem=ss, recv_sem=rs,
            device_id=device, device_id_type=MESH,
        )
        copy.start()
        sends.append(copy)
        return copy

    def cols(j):
        return pl.ds(j * width, width)

    def norms(block):
        wide = block.astype(jnp.float32)
        return jnp.sum(wide * wide, axis=1, keepdims=True)

    def soften(scores):
        top = jnp.max(scores, axis=0, keepdims=True)
        lifted = jnp.exp(scores - top)
        return top, lifted, jnp.sum(lifted, axis=0, keepdims=True)

    def combine(found):
        all_top = found[0][0]
        for top, _ in found[1:]:
            all_top = jnp.maximum(all_top, top)
        all_total = found[0][1] * jnp.exp(found[0][0] - all_top)
        for top, total in found[1:]:
            all_total = all_total + total * jnp.exp(top - all_top)
        return all_top, all_total

    def send_stats(it, send, recv):
        return {
            slot: remote(
                send, recv.at[slot], stat_ss.at[it, slot], stat_rs.at[it, slot], device
            )
            for slot, _, device in column
        }

    for load in loads:
        load.wait()
    st1[...] = lax.dot_general(
        cs[...], xs[my_rows, :], NT, preferred_element_type=jnp.float32
    ) - 0.5 * norms(cs[...])
    pl.semaphore_wait(barrier, len(column) + 3)
    top, lifted, total = soften(st1[...])
    stat_send1[0:1, :] = top
    stat_send1[1:2, :] = total
    arrivals = send_stats(0, stat_send1, stat_recv1)
    st1[...] = lifted
    lifted_flight = remote(st1.at[other_half], er, e_ss.at[0], e_rs.at[0], (sibling, z))
    x_flights = [
        remote(
            xs.at[my_rows, cols(j)], xs.at[my_rows, cols(j)],
            x_ss.at[j], x_rs.at[j], (sibling, z),
        )
        for j in range(chunks)
    ]

    for it in range(ITERS):
        if it == 0:
            for slot, _, _ in column:
                arrivals[slot].wait_recv()
            stats = [
                (flip, (stat_recv1[slot, 0:1, :], stat_recv1[slot, 1:2, :]))
                for slot, flip, _ in sorted(column, key=lambda entry: entry[0])
            ]
            own = [(top, total)] + [found for flip, found in stats if flip == 0]
            others = [found for flip, found in stats if flip == 1]
            all_top, all_total = combine(own)
            energy_ref[...] = all_top + jnp.log(all_total)
            scale = jnp.exp(top - all_top) / all_total
            wt[:, my_rows] = (st1[my_half, :] * scale).astype(jnp.bfloat16)
            all_top, all_total = combine(others)
            scale = jnp.exp(others[0][0] - all_top) / all_total
            lifted_flight.wait_recv()
            wt[:, other_rows] = (er[...] * scale).astype(jnp.bfloat16)
        else:
            top, lifted, total = soften(st2[...] - 0.5 * sq[...])
            stat_send2[0:1, :] = top
            stat_send2[1:2, :] = total
            arrivals = send_stats(1, stat_send2, stat_recv2)
            st2[...] = lifted
            for slot, _, _ in column:
                arrivals[slot].wait_recv()
            all_top, all_total = combine(
                [(top, total)]
                + [(stat_recv2[s, 0:1, :], stat_recv2[s, 1:2, :]) for s, _, _ in column]
            )
            scale = jnp.exp(top - all_top) / all_total
            wt[...] = (st2[...] * scale).astype(jnp.bfloat16)

        outs = []
        masses = []
        flights = {}

        def sums(j, it=it):
            if it == 0:
                x_flights[j].wait_recv()
            both = jnp.dot(wt[...], xs[:, cols(j)], preferred_element_type=jnp.float32)
            k0[j] = both
            s1[it, j] = both.astype(jnp.bfloat16)
            for p in (2, 0, 1):
                flights[1 + p, j] = remote(
                    s1.at[it, j, part(chip + flips[p])], r1.at[it, j, p],
                    ring_ss.at[it, j, 1 + p], ring_rs.at[it, j, 1 + p],
                    (r + 2 * flips[p], z),
                )

        def send_masses(it=it):
            mass_send[it] = lax.dot_general(
                jnp.ones((8, 2 * rows), jnp.bfloat16), wt[...], NT,
                preferred_element_type=jnp.float32,
            )[0:1, :]
            for p in range(3):
                masses.append(
                    remote(
                        mass_send.at[it], mass_recv.at[it, p],
                        mass_ss.at[it, p], mass_rs.at[it, p],
                        (r + 2 * flips[p], z),
                    )
                )

        def take_masses(it=it):
            everyone = mass_send[it]
            for p in range(3):
                masses[p].wait_recv()
                everyone = everyone + mass_recv[it, p]
            tall = jnp.broadcast_to(everyone, (128, half))
            mass_col[...] = 1.0 / (jnp.transpose(tall) + PRIOR_WEIGHT)

        def save(j, n, rows_of, it=it):
            copy = pltpu.make_async_copy(
                cc.at[it, j, rows_of], out_hbm.at[rows_of, cols(j)], out_sem.at[j, n]
            )
            copy.start()
            outs.append(copy)

        def share_out(j, n, here, it=it):
            spot = cc.at[it, j, here]
            flights[7 + n, j] = remote(
                spot, spot, ring_ss.at[it, j, 7 + n], ring_rs.at[it, j, 7 + n], (sibling, z)
            )
            save(j, n, here)

        def update(j, it=it):
            mine = place(core, chip)
            old = cs[mine, cols(j)] if it == 0 else cc[it - 1, j, mine]
            blend = k0[j, part(chip)] + PRIOR_WEIGHT * old.astype(jnp.float32)
            for p in range(3):
                flights[1 + p, j].wait_recv()
                blend = blend + r1[it, j, p].astype(jnp.float32)
            cc[it, j, mine] = (blend * mass_col[part(chip), 0:1]).astype(jnp.bfloat16)
            here = cc.at[it, j, mine]
            for p in (2, 0, 1):
                flights[4 + p, j] = remote(
                    here, here, ring_ss.at[it, j, 4 + p], ring_rs.at[it, j, 4 + p],
                    (r + 2 * flips[p], z),
                )
            if it == ITERS - 1:
                share_out(j, 0, mine)

        def gather(j, it=it):
            for p in range(3):
                flights[4 + p, j].wait_recv()
                if it == ITERS - 1:
                    share_out(j, 1 + p, place(core, chip + flips[p]))
            if it < ITERS - 1:
                block = cc[it, j, my_half]
                inner = lax.dot_general(
                    block, xs[:, cols(j)], NT, preferred_element_type=jnp.float32
                )
                if j == 0:
                    st2[...] = inner
                    sq[...] = norms(block)
                else:
                    st2[...] += inner
                    sq[...] += norms(block)

        def finish(j):
            for p, flip in enumerate((0,) + flips):
                flights[7 + p, j].wait_recv()
                save(j, 4 + p, place(1 - core, chip + flip))

        for j in range(chunks):
            sums(j)
            if j == 0:
                send_masses()
        take_masses()
        for j in range(chunks):
            update(j)
        for j in range(chunks):
            gather(j)
        if it == ITERS - 1:
            for j in range(chunks):
                finish(j)
        for copy in outs:
            copy.wait()

    for copy in sends:
        copy.wait_send()


def local_fused(groups, embeddings, centroids):
    rows, depth = embeddings.shape
    count = centroids.shape[0]
    chunks = CHUNKS
    width = depth // chunks
    half, share = count // 2, count // 8
    peers = 2 * groups - 1
    bf16, f32 = jnp.bfloat16, jnp.float32
    dma = pltpu.SemaphoreType.DMA
    result, energy = pl.pallas_call(
        functools.partial(kernel, groups, chunks),
        out_shape=(
            jax.ShapeDtypeStruct((count, depth), bf16),
            jax.ShapeDtypeStruct((1, rows), f32),
        ),
        in_specs=[pl.BlockSpec(memory_space=pl.ANY)] * 2,
        out_specs=(
            pl.BlockSpec(memory_space=pl.ANY),
            pl.BlockSpec(memory_space=pltpu.VMEM),
        ),
        scratch_shapes=[
            pltpu.VMEM((2 * rows, depth), bf16),
            pltpu.VMEM((count, depth), bf16),
            pltpu.VMEM((half, 2 * rows), bf16),
            pltpu.VMEM((count, rows), f32),
            pltpu.VMEM((half, rows), f32),
            pltpu.VMEM((half, 2 * rows), f32),
            pltpu.VMEM((half, 1), f32),
            pltpu.VMEM((half, 128), f32),
            pltpu.VMEM((2, rows), f32),
            pltpu.VMEM((peers, 2, rows), f32),
            pltpu.VMEM((2, 2 * rows), f32),
            pltpu.VMEM((peers, 2, 2 * rows), f32),
            pltpu.VMEM((ITERS, 1, half), f32),
            pltpu.VMEM((ITERS, 3, 1, half), f32),
            pltpu.VMEM((chunks, half, width), f32),
            pltpu.VMEM((ITERS, chunks, half, width), bf16),
            pltpu.VMEM((ITERS, chunks, 3, share, width), bf16),
            pltpu.VMEM((ITERS, chunks, count, width), bf16),
            dma((2,)),
            dma((chunks, 8)),
            dma((chunks,)),
            dma((chunks,)),
            dma((1,)),
            dma((1,)),
            dma((ITERS, peers)),
            dma((ITERS, peers)),
            dma((ITERS, 3)),
            dma((ITERS, 3)),
            dma((ITERS, chunks, 11)),
            dma((ITERS, chunks, 11)),
        ],
        compiler_params=pltpu.CompilerParams(
            collective_id=0, has_side_effects=True, vmem_limit_bytes=63 * 1024 * 1024
        ),
        cost_estimate=pl.CostEstimate(
            flops=8 * rows * count * depth,
            bytes_accessed=2 * depth * (rows + 2 * count),
            transcendentals=2 * rows * count,
        ),
    )(embeddings, centroids)
    return result, energy.reshape(rows)


def solution(mesh):
    def local(embeddings, centroids):
        rows, depth = embeddings.shape
        count = centroids.shape[0]
        groups = mesh.shape["cent"]
        fits = (
            mesh.shape["row"] == 8
            and groups > 1
            and rows % 256 == 0
            and rows <= 1024
            and count == 256
            and depth % (128 * CHUNKS) == 0
        )
        if fits:
            return local_fused(groups, embeddings, centroids)
        return local_plain(embeddings, centroids)

    return jax.shard_map(
        local,
        mesh=mesh,
        in_specs=(P("row", None), P("cent", None)),
        out_specs=(P("cent", None), P("row")),
        check_vma=False,
    )
```

```python
import functools

import jax
import jax.numpy as jnp
from jax import lax
from jax.experimental import pallas as pl
from jax.experimental.pallas import tpu as pltpu
from jax.sharding import PartitionSpec as P

ITERS = 2
PRIOR_WEIGHT = 8.0
CHUNKS = 3
MESH = pl.DeviceIdType.MESH
NT = (((1,), (1,)), ((), ()))


def score_against(embeddings, cluster_block):
    squared = jnp.sum(jnp.square(cluster_block.astype(jnp.float32)), axis=1)
    inner = lax.dot_general(embeddings, cluster_block, NT, preferred_element_type=jnp.float32)
    return inner - 0.5 * squared[None, :]


def updated_rows(totals, mass, previous):
    blended = (totals + PRIOR_WEIGHT * previous.astype(jnp.float32)) / (mass + PRIOR_WEIGHT)[
        :, None
    ]
    return blended.astype(jnp.bfloat16)


def local_plain(embeddings, centroids):
    row_count = embeddings.shape[0]
    cluster_count = centroids.shape[0]
    share_rows = cluster_count // lax.axis_size("row")
    shares = lax.dynamic_slice_in_dim(centroids, lax.axis_index("row") * share_rows, share_rows, 0)
    energy = jnp.zeros((row_count,), jnp.float32)
    for iteration in range(ITERS):
        if iteration == 0:
            scores = score_against(embeddings, centroids)
        else:
            scores = score_against(embeddings, lax.all_gather(shares, "row", axis=0, tiled=True))
        row_top = lax.pmax(jnp.max(scores, axis=1), "cent")
        lifted = jnp.exp(scores - row_top[:, None])
        row_total = lax.psum(jnp.sum(lifted, axis=1), "cent")
        weights = (lifted / row_total[:, None]).astype(jnp.bfloat16)
        totals = lax.dot_general(
            weights, embeddings, (((0,), (0,)), ((), ())), preferred_element_type=jnp.float32
        )
        mass = jnp.sum(weights.astype(jnp.float32), axis=0)
        energies = row_top + jnp.log(row_total)
        if iteration == 0:
            energy = energies
        share_totals, share_mass = (
            lax.psum_scatter(totals, "row", scatter_dimension=0, tiled=True),
            lax.psum_scatter(mass, "row", scatter_dimension=0, tiled=True),
        )
        shares = updated_rows(share_totals, share_mass, shares)
    result = lax.all_gather(shares, "row", axis=0, tiled=True)
    return (result, energy)


def kernel(
    groups, chunks,
    x_hbm, c_hbm, out_hbm, energy_ref,
    xs, cs, wt, st1, er, st2, sq, mass_col,
    stat_send1, stat_recv1, stat_send2, stat_recv2, mass_send, mass_recv,
    k0, s1, r1, cc,
    load_sem, out_sem, x_ss, x_rs, e_ss, e_rs, stat_ss, stat_rs, mass_ss, mass_rs,
    ring_ss, ring_rs,
):
    rows, depth = x_hbm.shape
    count = cs.shape[0]
    width = depth // chunks
    half, share = count // 2, count // 8
    r = lax.axis_index("row")
    z = lax.axis_index("cent")
    core = lax.rem(r, 2)
    px = lax.rem(r // 2, 2)
    py = r // 4
    sibling = r + 1 - 2 * core
    flips = (1 - 2 * px, 2 * (1 - 2 * py), 1 - 2 * px + 2 * (1 - 2 * py))
    chip = r // 2
    my_half = pl.ds(pl.multiple_of(core * half, half), half)
    other_half = pl.ds(pl.multiple_of((1 - core) * half, half), half)
    my_rows = pl.ds(pl.multiple_of(core * rows, rows), rows)
    other_rows = pl.ds(pl.multiple_of((1 - core) * rows, rows), rows)

    def part(owner):
        return pl.ds(pl.multiple_of(owner * share, share), share)

    def place(core_of, owner):
        return pl.ds(pl.multiple_of(core_of * half + owner * share, share), share)

    column = [
        (2 * d + flip - 1, flip, (r + flip * (1 - 2 * core), lax.rem(z + d, groups)))
        for d in range(groups)
        for flip in range(2)
        if d + flip > 0
    ]
    column = sorted(column, key=lambda entry: -entry[0])

    barrier = pltpu.get_barrier_semaphore()
    for _, _, device in column:
        pl.semaphore_signal(barrier, inc=1, device_id=device, device_id_type=MESH)
    for p in range(3):
        pl.semaphore_signal(
            barrier, inc=1, device_id=(r + 2 * flips[p], z), device_id_type=MESH
        )
    loads = [
        pltpu.make_async_copy(x_hbm, xs.at[my_rows], load_sem.at[0]),
        pltpu.make_async_copy(c_hbm, cs, load_sem.at[1]),
    ]
    for load in loads:
        load.start()

    sends = []

    def remote(src, dst, ss, rs, device):
        copy = pltpu.make_async_remote_copy(
            src_ref=src, dst_ref=dst, send_sem=ss, recv_sem=rs,
            device_id=device, device_id_type=MESH,
        )
        copy.start()
        sends.append(copy)
        return copy

    def cols(j):
        return pl.ds(j * width, width)

    def norms(block):
        wide = block.astype(jnp.float32)
        return jnp.sum(wide * wide, axis=1, keepdims=True)

    def soften(scores):
        top = jnp.max(scores, axis=0, keepdims=True)
        lifted = jnp.exp(scores - top)
        return top, lifted, jnp.sum(lifted, axis=0, keepdims=True)

    def combine(found):
        all_top = found[0][0]
        for top, _ in found[1:]:
            all_top = jnp.maximum(all_top, top)
        all_total = found[0][1] * jnp.exp(found[0][0] - all_top)
        for top, total in found[1:]:
            all_total = all_total + total * jnp.exp(top - all_top)
        return all_top, all_total

    def send_stats(it, send, recv):
        return {
            slot: remote(
                send, recv.at[slot], stat_ss.at[it, slot], stat_rs.at[it, slot], device
            )
            for slot, _, device in column
        }

    for load in loads:
        load.wait()
    st1[...] = lax.dot_general(
        cs[...], xs[my_rows, :], NT, preferred_element_type=jnp.float32
    ) - 0.5 * norms(cs[...])
    pl.semaphore_wait(barrier, len(column) + 3)
    top, lifted, total = soften(st1[...])
    stat_send1[0:1, :] = top
    stat_send1[1:2, :] = total
    arrivals = send_stats(0, stat_send1, stat_recv1)
    st1[...] = lifted
    lifted_flight = remote(st1.at[other_half], er, e_ss.at[0], e_rs.at[0], (sibling, z))
    x_flights = [
        remote(
            xs.at[my_rows, cols(j)], xs.at[my_rows, cols(j)],
            x_ss.at[j], x_rs.at[j], (sibling, z),
        )
        for j in range(chunks)
    ]

    for it in range(ITERS):
        if it == 0:
            for slot, _, _ in column:
                arrivals[slot].wait_recv()
            stats = [
                (flip, (stat_recv1[slot, 0:1, :], stat_recv1[slot, 1:2, :]))
                for slot, flip, _ in sorted(column, key=lambda entry: entry[0])
            ]
            own = [(top, total)] + [found for flip, found in stats if flip == 0]
            others = [found for flip, found in stats if flip == 1]
            all_top, all_total = combine(own)
            energy_ref[...] = all_top + jnp.log(all_total)
            scale = jnp.exp(top - all_top) / all_total
            wt[:, my_rows] = (st1[my_half, :] * scale).astype(jnp.bfloat16)
            all_top, all_total = combine(others)
            scale = jnp.exp(others[0][0] - all_top) / all_total
            lifted_flight.wait_recv()
            wt[:, other_rows] = (er[...] * scale).astype(jnp.bfloat16)
        else:
            top, lifted, total = soften(st2[...] - 0.5 * sq[...])
            stat_send2[0:1, :] = top
            stat_send2[1:2, :] = total
            arrivals = send_stats(1, stat_send2, stat_recv2)
            st2[...] = lifted
            for slot, _, _ in column:
                arrivals[slot].wait_recv()
            all_top, all_total = combine(
                [(top, total)]
                + [(stat_recv2[s, 0:1, :], stat_recv2[s, 1:2, :]) for s, _, _ in column]
            )
            scale = jnp.exp(top - all_top) / all_total
            wt[...] = (st2[...] * scale).astype(jnp.bfloat16)

        outs = []
        masses = []
        flights = {}

        def sums(j, it=it):
            if it == 0:
                x_flights[j].wait_recv()
            both = jnp.dot(wt[...], xs[:, cols(j)], preferred_element_type=jnp.float32)
            k0[j] = both
            s1[it, j] = both.astype(jnp.bfloat16)
            for p in (2, 0, 1):
                flights[1 + p, j] = remote(
                    s1.at[it, j, part(chip + flips[p])], r1.at[it, j, p],
                    ring_ss.at[it, j, 1 + p], ring_rs.at[it, j, 1 + p],
                    (r + 2 * flips[p], z),
                )

        def send_masses(it=it):
            mass_send[it] = lax.dot_general(
                jnp.ones((8, 2 * rows), jnp.bfloat16), wt[...], NT,
                preferred_element_type=jnp.float32,
            )[0:1, :]
            for p in range(3):
                masses.append(
                    remote(
                        mass_send.at[it], mass_recv.at[it, p],
                        mass_ss.at[it, p], mass_rs.at[it, p],
                        (r + 2 * flips[p], z),
                    )
                )

        def take_masses(it=it):
            everyone = mass_send[it]
            for p in range(3):
                masses[p].wait_recv()
                everyone = everyone + mass_recv[it, p]
            tall = jnp.broadcast_to(everyone, (128, half))
            mass_col[...] = 1.0 / (jnp.transpose(tall) + PRIOR_WEIGHT)

        def save(j, n, rows_of, it=it):
            copy = pltpu.make_async_copy(
                cc.at[it, j, rows_of], out_hbm.at[rows_of, cols(j)], out_sem.at[j, n]
            )
            copy.start()
            outs.append(copy)

        def share_out(j, n, here, it=it):
            spot = cc.at[it, j, here]
            flights[7 + n, j] = remote(
                spot, spot, ring_ss.at[it, j, 7 + n], ring_rs.at[it, j, 7 + n], (sibling, z)
            )
            save(j, n, here)

        def update(j, it=it):
            mine = place(core, chip)
            old = cs[mine, cols(j)] if it == 0 else cc[it - 1, j, mine]
            blend = k0[j, part(chip)] + PRIOR_WEIGHT * old.astype(jnp.float32)
            for p in range(3):
                flights[1 + p, j].wait_recv()
                blend = blend + r1[it, j, p].astype(jnp.float32)
            cc[it, j, mine] = (blend * mass_col[part(chip), 0:1]).astype(jnp.bfloat16)
            here = cc.at[it, j, mine]
            for p in (2, 0, 1):
                flights[4 + p, j] = remote(
                    here, here, ring_ss.at[it, j, 4 + p], ring_rs.at[it, j, 4 + p],
                    (r + 2 * flips[p], z),
                )
            if it == ITERS - 1:
                share_out(j, 0, mine)

        def gather(j, it=it):
            for p in range(3):
                flights[4 + p, j].wait_recv()
                if it == ITERS - 1:
                    share_out(j, 1 + p, place(core, chip + flips[p]))
            if it < ITERS - 1:
                block = cc[it, j, my_half]
                inner = lax.dot_general(
                    block, xs[:, cols(j)], NT, preferred_element_type=jnp.float32
                )
                if j == 0:
                    st2[...] = inner
                    sq[...] = norms(block)
                else:
                    st2[...] += inner
                    sq[...] += norms(block)

        def finish(j):
            for p, flip in enumerate((0,) + flips):
                flights[7 + p, j].wait_recv()
                save(j, 4 + p, place(1 - core, chip + flip))

        for j in range(chunks):
            sums(j)
            if j == 0:
                send_masses()
        take_masses()
        for j in range(chunks):
            update(j)
        for j in range(chunks):
            gather(j)
        if it == ITERS - 1:
            for j in range(chunks):
                finish(j)
        for copy in outs:
            copy.wait()

    for copy in sends:
        copy.wait_send()


def local_fused(groups, embeddings, centroids):
    rows, depth = embeddings.shape
    count = centroids.shape[0]
    chunks = CHUNKS
    width = depth // chunks
    half, share = count // 2, count // 8
    peers = 2 * groups - 1
    bf16, f32 = jnp.bfloat16, jnp.float32
    dma = pltpu.SemaphoreType.DMA
    result, energy = pl.pallas_call(
        functools.partial(kernel, groups, chunks),
        out_shape=(
            pltpu.VMEM((count, depth), bf16),
            pltpu.VMEM((1, rows), f32),
        ),
        in_specs=[pl.BlockSpec(memory_space=pl.ANY)] * 2,
        out_specs=(
            pl.BlockSpec(memory_space=pl.ANY),
            pl.BlockSpec(memory_space=pltpu.VMEM),
        ),
        scratch_shapes=[
            pltpu.VMEM((2 * rows, depth), bf16),
            pltpu.VMEM((count, depth), bf16),
            pltpu.VMEM((half, 2 * rows), bf16),
            pltpu.VMEM((count, rows), f32),
            pltpu.VMEM((half, rows), f32),
            pltpu.VMEM((half, 2 * rows), f32),
            pltpu.VMEM((half, 1), f32),
            pltpu.VMEM((half, 128), f32),
            pltpu.VMEM((2, rows), f32),
            pltpu.VMEM((peers, 2, rows), f32),
            pltpu.VMEM((2, 2 * rows), f32),
            pltpu.VMEM((peers, 2, 2 * rows), f32),
            pltpu.VMEM((ITERS, 1, half), f32),
            pltpu.VMEM((ITERS, 3, 1, half), f32),
            pltpu.VMEM((chunks, half, width), f32),
            pltpu.VMEM((ITERS, chunks, half, width), bf16),
            pltpu.VMEM((ITERS, chunks, 3, share, width), bf16),
            pltpu.VMEM((ITERS, chunks, count, width), bf16),
            dma((2,)),
            dma((chunks, 8)),
            dma((chunks,)),
            dma((chunks,)),
            dma((1,)),
            dma((1,)),
            dma((ITERS, peers)),
            dma((ITERS, peers)),
            dma((ITERS, 3)),
            dma((ITERS, 3)),
            dma((ITERS, chunks, 11)),
            dma((ITERS, chunks, 11)),
        ],
        compiler_params=pltpu.CompilerParams(
            collective_id=0, has_side_effects=True, vmem_limit_bytes=63 * 1024 * 1024
        ),
        cost_estimate=pl.CostEstimate(
            flops=8 * rows * count * depth,
            bytes_accessed=2 * depth * (rows + 2 * count),
            transcendentals=2 * rows * count,
        ),
    )(embeddings, centroids)
    return result, energy.reshape(rows)


def solution(mesh):
    def local(embeddings, centroids):
        rows, depth = embeddings.shape
        count = centroids.shape[0]
        groups = mesh.shape["cent"]
        fits = (
            mesh.shape["row"] == 8
            and groups > 1
            and rows % 256 == 0
            and rows <= 1024
            and count == 256
            and depth % (128 * CHUNKS) == 0
        )
        if fits:
            return local_fused(groups, embeddings, centroids)
        return local_plain(embeddings, centroids)

    return jax.shard_map(
        local,
        mesh=mesh,
        in_specs=(P("row", None), P("cent", None)),
        out_specs=(P("cent", None), P("row")),
        check_vma=False,
    )
```

```python
import functools

import jax
import jax.numpy as jnp
from jax import lax
from jax.experimental import pallas as pl
from jax.experimental.pallas import tpu as pltpu
from jax.sharding import PartitionSpec as P

ITERS = 2
PRIOR_WEIGHT = 8.0
CHUNKS = 3
MESH = pl.DeviceIdType.MESH
NT = (((1,), (1,)), ((), ()))


def score_against(embeddings, cluster_block):
    squared = jnp.sum(jnp.square(cluster_block.astype(jnp.float32)), axis=1)
    inner = lax.dot_general(embeddings, cluster_block, NT, preferred_element_type=jnp.float32)
    return inner - 0.5 * squared[None, :]


def updated_rows(totals, mass, previous):
    blended = (totals + PRIOR_WEIGHT * previous.astype(jnp.float32)) / (mass + PRIOR_WEIGHT)[
        :, None
    ]
    return blended.astype(jnp.bfloat16)


def local_plain(embeddings, centroids):
    row_count = embeddings.shape[0]
    cluster_count = centroids.shape[0]
    share_rows = cluster_count // lax.axis_size("row")
    shares = lax.dynamic_slice_in_dim(centroids, lax.axis_index("row") * share_rows, share_rows, 0)
    energy = jnp.zeros((row_count,), jnp.float32)
    for iteration in range(ITERS):
        if iteration == 0:
            scores = score_against(embeddings, centroids)
        else:
            scores = score_against(embeddings, lax.all_gather(shares, "row", axis=0, tiled=True))
        row_top = lax.pmax(jnp.max(scores, axis=1), "cent")
        lifted = jnp.exp(scores - row_top[:, None])
        row_total = lax.psum(jnp.sum(lifted, axis=1), "cent")
        weights = (lifted / row_total[:, None]).astype(jnp.bfloat16)
        totals = lax.dot_general(
            weights, embeddings, (((0,), (0,)), ((), ())), preferred_element_type=jnp.float32
        )
        mass = jnp.sum(weights.astype(jnp.float32), axis=0)
        energies = row_top + jnp.log(row_total)
        if iteration == 0:
            energy = energies
        share_totals, share_mass = (
            lax.psum_scatter(totals, "row", scatter_dimension=0, tiled=True),
            lax.psum_scatter(mass, "row", scatter_dimension=0, tiled=True),
        )
        shares = updated_rows(share_totals, share_mass, shares)
    result = lax.all_gather(shares, "row", axis=0, tiled=True)
    return (result, energy)


def kernel(
    groups, chunks,
    x_hbm, c_hbm, out_ref, energy_ref,
    xs, cs, wt, st1, er, st2, sq, mass_col,
    stat_send1, stat_recv1, stat_send2, stat_recv2, mass_send, mass_recv,
    k0, s1, r1, cc,
    load_sem, x_ss, x_rs, e_ss, e_rs, stat_ss, stat_rs, mass_ss, mass_rs,
    ring_ss, ring_rs,
):
    rows, depth = x_hbm.shape
    count = cs.shape[0]
    width = depth // chunks
    half, share = count // 2, count // 8
    r = lax.axis_index("row")
    z = lax.axis_index("cent")
    core = lax.rem(r, 2)
    px = lax.rem(r // 2, 2)
    py = r // 4
    sibling = r + 1 - 2 * core
    flips = (1 - 2 * px, 2 * (1 - 2 * py), 1 - 2 * px + 2 * (1 - 2 * py))
    chip = r // 2
    my_half = pl.ds(pl.multiple_of(core * half, half), half)
    other_half = pl.ds(pl.multiple_of((1 - core) * half, half), half)
    my_rows = pl.ds(pl.multiple_of(core * rows, rows), rows)
    other_rows = pl.ds(pl.multiple_of((1 - core) * rows, rows), rows)

    def part(owner):
        return pl.ds(pl.multiple_of(owner * share, share), share)

    def place(core_of, owner):
        return pl.ds(pl.multiple_of(core_of * half + owner * share, share), share)

    column = [
        (2 * d + flip - 1, flip, (r + flip * (1 - 2 * core), lax.rem(z + d, groups)))
        for d in range(groups)
        for flip in range(2)
        if d + flip > 0
    ]
    column = sorted(column, key=lambda entry: -entry[0])

    barrier = pltpu.get_barrier_semaphore()
    for _, _, device in column:
        pl.semaphore_signal(barrier, inc=1, device_id=device, device_id_type=MESH)
    for p in range(3):
        pl.semaphore_signal(
            barrier, inc=1, device_id=(r + 2 * flips[p], z), device_id_type=MESH
        )
    loads = [
        pltpu.make_async_copy(x_hbm, xs.at[my_rows], load_sem.at[0]),
        pltpu.make_async_copy(c_hbm, cs, load_sem.at[1]),
    ]
    for load in loads:
        load.start()

    sends = []

    def remote(src, dst, ss, rs, device):
        copy = pltpu.make_async_remote_copy(
            src_ref=src, dst_ref=dst, send_sem=ss, recv_sem=rs,
            device_id=device, device_id_type=MESH,
        )
        copy.start()
        sends.append(copy)
        return copy

    def cols(j):
        return pl.ds(j * width, width)

    def norms(block):
        wide = block.astype(jnp.float32)
        return jnp.sum(wide * wide, axis=1, keepdims=True)

    def soften(scores):
        top = jnp.max(scores, axis=0, keepdims=True)
        lifted = jnp.exp(scores - top)
        return top, lifted, jnp.sum(lifted, axis=0, keepdims=True)

    def combine(found):
        all_top = found[0][0]
        for top, _ in found[1:]:
            all_top = jnp.maximum(all_top, top)
        all_total = found[0][1] * jnp.exp(found[0][0] - all_top)
        for top, total in found[1:]:
            all_total = all_total + total * jnp.exp(top - all_top)
        return all_top, all_total

    def send_stats(it, send, recv):
        return {
            slot: remote(
                send, recv.at[slot], stat_ss.at[it, slot], stat_rs.at[it, slot], device
            )
            for slot, _, device in column
        }

    for load in loads:
        load.wait()
    st1[...] = lax.dot_general(
        cs[...], xs[my_rows, :], NT, preferred_element_type=jnp.float32
    ) - 0.5 * norms(cs[...])
    pl.semaphore_wait(barrier, len(column) + 3)
    top, lifted, total = soften(st1[...])
    stat_send1[0:1, :] = top
    stat_send1[1:2, :] = total
    arrivals = send_stats(0, stat_send1, stat_recv1)
    st1[...] = lifted
    lifted_flight = remote(st1.at[other_half], er, e_ss.at[0], e_rs.at[0], (sibling, z))
    x_flights = [
        remote(
            xs.at[my_rows, cols(j)], xs.at[my_rows, cols(j)],
            x_ss.at[j], x_rs.at[j], (sibling, z),
        )
        for j in range(chunks)
    ]

    for it in range(ITERS):
        if it == 0:
            for slot, _, _ in column:
                arrivals[slot].wait_recv()
            stats = [
                (flip, (stat_recv1[slot, 0:1, :], stat_recv1[slot, 1:2, :]))
                for slot, flip, _ in sorted(column, key=lambda entry: entry[0])
            ]
            own = [(top, total)] + [found for flip, found in stats if flip == 0]
            others = [found for flip, found in stats if flip == 1]
            all_top, all_total = combine(own)
            energy_parts = (all_top, all_total)
            scale = jnp.exp(top - all_top) / all_total
            wt[:, my_rows] = (st1[my_half, :] * scale).astype(jnp.bfloat16)
            all_top, all_total = combine(others)
            scale = jnp.exp(others[0][0] - all_top) / all_total
            lifted_flight.wait_recv()
            wt[:, other_rows] = (er[...] * scale).astype(jnp.bfloat16)
        else:
            top, lifted, total = soften(st2[...] - 0.5 * sq[...])
            stat_send2[0:1, :] = top
            stat_send2[1:2, :] = total
            arrivals = send_stats(1, stat_send2, stat_recv2)
            st2[...] = lifted
            for slot, _, _ in column:
                arrivals[slot].wait_recv()
            all_top, all_total = combine(
                [(top, total)]
                + [(stat_recv2[s, 0:1, :], stat_recv2[s, 1:2, :]) for s, _, _ in column]
            )
            scale = jnp.exp(top - all_top) / all_total
            wt[...] = (st2[...] * scale).astype(jnp.bfloat16)

        masses = []
        flights = {}

        def sums(j, it=it):
            if it == 0:
                x_flights[j].wait_recv()
            both = jnp.dot(wt[...], xs[:, cols(j)], preferred_element_type=jnp.float32)
            k0[j] = both
            s1[it, j] = both.astype(jnp.bfloat16)
            for p in (2, 0, 1):
                flights[1 + p, j] = remote(
                    s1.at[it, j, part(chip + flips[p])], r1.at[it, j, p],
                    ring_ss.at[it, j, 1 + p], ring_rs.at[it, j, 1 + p],
                    (r + 2 * flips[p], z),
                )

        def send_masses(it=it):
            mass_send[it] = lax.dot_general(
                jnp.ones((8, 2 * rows), jnp.bfloat16), wt[...], NT,
                preferred_element_type=jnp.float32,
            )[0:1, :]
            for p in range(3):
                masses.append(
                    remote(
                        mass_send.at[it], mass_recv.at[it, p],
                        mass_ss.at[it, p], mass_rs.at[it, p],
                        (r + 2 * flips[p], z),
                    )
                )

        def take_masses(it=it):
            everyone = mass_send[it]
            for p in range(3):
                masses[p].wait_recv()
                everyone = everyone + mass_recv[it, p]
            tall = jnp.broadcast_to(everyone, (128, half))
            mass_col[...] = 1.0 / (jnp.transpose(tall) + PRIOR_WEIGHT)

        def spot(j, rows_of, it=it):
            if it == ITERS - 1:
                return out_ref.at[rows_of, cols(j)]
            return cc.at[it, j, rows_of]

        def share_out(j, n, here, it=it):
            block = spot(j, here)
            flights[7 + n, j] = remote(
                block, block, ring_ss.at[it, j, 7 + n], ring_rs.at[it, j, 7 + n], (sibling, z)
            )

        def update(j, it=it):
            mine = place(core, chip)
            old = cs[mine, cols(j)] if it == 0 else cc[it - 1, j, mine]
            blend = k0[j, part(chip)] + PRIOR_WEIGHT * old.astype(jnp.float32)
            for p in range(3):
                flights[1 + p, j].wait_recv()
                blend = blend + r1[it, j, p].astype(jnp.float32)
            here = spot(j, mine)
            here[...] = (blend * mass_col[part(chip), 0:1]).astype(jnp.bfloat16)
            for p in (2, 0, 1):
                flights[4 + p, j] = remote(
                    here, here, ring_ss.at[it, j, 4 + p], ring_rs.at[it, j, 4 + p],
                    (r + 2 * flips[p], z),
                )
            if it == ITERS - 1:
                share_out(j, 0, mine)

        def gather(j, it=it):
            for p in range(3):
                flights[4 + p, j].wait_recv()
                if it == ITERS - 1:
                    share_out(j, 1 + p, place(core, chip + flips[p]))
            if it < ITERS - 1:
                block = cc[it, j, my_half]
                inner = lax.dot_general(
                    block, xs[:, cols(j)], NT, preferred_element_type=jnp.float32
                )
                if j == 0:
                    st2[...] = inner
                    sq[...] = norms(block)
                else:
                    st2[...] += inner
                    sq[...] += norms(block)

        def finish(j):
            for p in range(4):
                flights[7 + p, j].wait_recv()

        for j in range(chunks):
            sums(j)
            if j == 0:
                send_masses()
        if it == 0:
            energy_ref[...] = energy_parts[0] + jnp.log(energy_parts[1])
        take_masses()
        for j in range(chunks):
            update(j)
        for j in range(chunks):
            gather(j)
        if it == ITERS - 1:
            for j in range(chunks):
                finish(j)

    for copy in sends:
        copy.wait_send()


def local_fused(groups, embeddings, centroids):
    rows, depth = embeddings.shape
    count = centroids.shape[0]
    chunks = CHUNKS
    width = depth // chunks
    half, share = count // 2, count // 8
    peers = 2 * groups - 1
    bf16, f32 = jnp.bfloat16, jnp.float32
    dma = pltpu.SemaphoreType.DMA
    result, energy = pl.pallas_call(
        functools.partial(kernel, groups, chunks),
        out_shape=(
            pltpu.VMEM((count, depth), bf16),
            pltpu.VMEM((1, rows), f32),
        ),
        in_specs=[pl.BlockSpec(memory_space=pl.ANY)] * 2,
        out_specs=(
            pl.BlockSpec(memory_space=pltpu.VMEM),
            pl.BlockSpec(memory_space=pltpu.VMEM),
        ),
        scratch_shapes=[
            pltpu.VMEM((2 * rows, depth), bf16),
            pltpu.VMEM((count, depth), bf16),
            pltpu.VMEM((half, 2 * rows), bf16),
            pltpu.VMEM((count, rows), f32),
            pltpu.VMEM((half, rows), f32),
            pltpu.VMEM((half, 2 * rows), f32),
            pltpu.VMEM((half, 1), f32),
            pltpu.VMEM((half, 128), f32),
            pltpu.VMEM((2, rows), f32),
            pltpu.VMEM((peers, 2, rows), f32),
            pltpu.VMEM((2, 2 * rows), f32),
            pltpu.VMEM((peers, 2, 2 * rows), f32),
            pltpu.VMEM((ITERS, 1, half), f32),
            pltpu.VMEM((ITERS, 3, 1, half), f32),
            pltpu.VMEM((chunks, half, width), f32),
            pltpu.VMEM((ITERS, chunks, half, width), bf16),
            pltpu.VMEM((ITERS, chunks, 3, share, width), bf16),
            pltpu.VMEM((ITERS - 1, chunks, count, width), bf16),
            dma((2,)),
            dma((chunks,)),
            dma((chunks,)),
            dma((1,)),
            dma((1,)),
            dma((ITERS, peers)),
            dma((ITERS, peers)),
            dma((ITERS, 3)),
            dma((ITERS, 3)),
            dma((ITERS, chunks, 11)),
            dma((ITERS, chunks, 11)),
        ],
        compiler_params=pltpu.CompilerParams(
            collective_id=0, has_side_effects=True, vmem_limit_bytes=63 * 1024 * 1024
        ),
        cost_estimate=pl.CostEstimate(
            flops=8 * rows * count * depth,
            bytes_accessed=2 * depth * (rows + 2 * count),
            transcendentals=2 * rows * count,
        ),
    )(embeddings, centroids)
    return result, energy.reshape(rows)


def solution(mesh):
    def local(embeddings, centroids):
        rows, depth = embeddings.shape
        count = centroids.shape[0]
        groups = mesh.shape["cent"]
        fits = (
            mesh.shape["row"] == 8
            and groups > 1
            and rows % 256 == 0
            and rows <= 1024
            and count == 256
            and depth % (128 * CHUNKS) == 0
        )
        if fits:
            return local_fused(groups, embeddings, centroids)
        return local_plain(embeddings, centroids)

    return jax.shard_map(
        local,
        mesh=mesh,
        in_specs=(P("row", None), P("cent", None)),
        out_specs=(P("cent", None), P("row")),
        check_vma=False,
    )
```

```python
import functools

import jax
import jax.numpy as jnp
from jax import lax
from jax.experimental import pallas as pl
from jax.experimental.pallas import tpu as pltpu
from jax.sharding import PartitionSpec as P

ITERS = 2
PRIOR_WEIGHT = 8.0
CHUNKS = 3
MESH = pl.DeviceIdType.MESH
NT = (((1,), (1,)), ((), ()))


def score_against(embeddings, cluster_block):
    squared = jnp.sum(jnp.square(cluster_block.astype(jnp.float32)), axis=1)
    inner = lax.dot_general(embeddings, cluster_block, NT, preferred_element_type=jnp.float32)
    return inner - 0.5 * squared[None, :]


def updated_rows(totals, mass, previous):
    blended = (totals + PRIOR_WEIGHT * previous.astype(jnp.float32)) / (mass + PRIOR_WEIGHT)[
        :, None
    ]
    return blended.astype(jnp.bfloat16)


def local_plain(embeddings, centroids):
    row_count = embeddings.shape[0]
    cluster_count = centroids.shape[0]
    share_rows = cluster_count // lax.axis_size("row")
    shares = lax.dynamic_slice_in_dim(centroids, lax.axis_index("row") * share_rows, share_rows, 0)
    energy = jnp.zeros((row_count,), jnp.float32)
    for iteration in range(ITERS):
        if iteration == 0:
            scores = score_against(embeddings, centroids)
        else:
            scores = score_against(embeddings, lax.all_gather(shares, "row", axis=0, tiled=True))
        row_top = lax.pmax(jnp.max(scores, axis=1), "cent")
        lifted = jnp.exp(scores - row_top[:, None])
        row_total = lax.psum(jnp.sum(lifted, axis=1), "cent")
        weights = (lifted / row_total[:, None]).astype(jnp.bfloat16)
        totals = lax.dot_general(
            weights, embeddings, (((0,), (0,)), ((), ())), preferred_element_type=jnp.float32
        )
        mass = jnp.sum(weights.astype(jnp.float32), axis=0)
        energies = row_top + jnp.log(row_total)
        if iteration == 0:
            energy = energies
        share_totals, share_mass = (
            lax.psum_scatter(totals, "row", scatter_dimension=0, tiled=True),
            lax.psum_scatter(mass, "row", scatter_dimension=0, tiled=True),
        )
        shares = updated_rows(share_totals, share_mass, shares)
    result = lax.all_gather(shares, "row", axis=0, tiled=True)
    return (result, energy)


def kernel(
    groups, chunks,
    x_hbm, c_hbm, out_ref, energy_ref,
    xs, cs, wt, st1, er, st2, sq, mass_col,
    stat_send1, stat_recv1, stat_send2, stat_recv2, mass_send, mass_recv,
    k0, s1, r1, cc,
    load_sem, x_ss, x_rs, e_ss, e_rs, stat_ss, stat_rs, mass_ss, mass_rs,
    ring_ss, ring_rs,
):
    rows, depth = x_hbm.shape
    count = cs.shape[0]
    width = depth // chunks
    half, share = count // 2, count // 8
    r = lax.axis_index("row")
    z = lax.axis_index("cent")
    core = lax.rem(r, 2)
    px = lax.rem(r // 2, 2)
    py = r // 4
    sibling = r + 1 - 2 * core
    flips = (1 - 2 * px, 2 * (1 - 2 * py), 1 - 2 * px + 2 * (1 - 2 * py))
    chip = r // 2
    my_half = pl.ds(pl.multiple_of(core * half, half), half)
    other_half = pl.ds(pl.multiple_of((1 - core) * half, half), half)
    my_rows = pl.ds(pl.multiple_of(core * rows, rows), rows)
    other_rows = pl.ds(pl.multiple_of((1 - core) * rows, rows), rows)

    def part(owner):
        return pl.ds(pl.multiple_of(owner * share, share), share)

    def place(core_of, owner):
        return pl.ds(pl.multiple_of(core_of * half + owner * share, share), share)

    column = [
        (2 * d + flip - 1, flip, (r + flip * (1 - 2 * core), lax.rem(z + d, groups)))
        for d in range(groups)
        for flip in range(2)
        if d + flip > 0
    ]
    column = sorted(column, key=lambda entry: -entry[0])

    barrier = pltpu.get_barrier_semaphore()
    for _, _, device in column:
        pl.semaphore_signal(barrier, inc=1, device_id=device, device_id_type=MESH)
    for p in range(3):
        pl.semaphore_signal(
            barrier, inc=1, device_id=(r + 2 * flips[p], z), device_id_type=MESH
        )
    loads = [
        pltpu.make_async_copy(x_hbm, xs.at[my_rows], load_sem.at[0]),
        pltpu.make_async_copy(c_hbm, cs, load_sem.at[1]),
    ]
    for load in loads:
        load.start()

    sends = []

    def remote(src, dst, ss, rs, device):
        copy = pltpu.make_async_remote_copy(
            src_ref=src, dst_ref=dst, send_sem=ss, recv_sem=rs,
            device_id=device, device_id_type=MESH,
        )
        copy.start()
        sends.append(copy)
        return copy

    def cols(j):
        return pl.ds(j * width, width)

    def norms(block):
        wide = block.astype(jnp.float32)
        return jnp.sum(wide * wide, axis=1, keepdims=True)

    def soften(scores):
        top = jnp.max(scores, axis=0, keepdims=True)
        lifted = jnp.exp(scores - top)
        return top, lifted, jnp.sum(lifted, axis=0, keepdims=True)

    def combine(found):
        all_top = found[0][0]
        for top, _ in found[1:]:
            all_top = jnp.maximum(all_top, top)
        all_total = found[0][1] * jnp.exp(found[0][0] - all_top)
        for top, total in found[1:]:
            all_total = all_total + total * jnp.exp(top - all_top)
        return all_top, all_total

    def send_stats(it, send, recv):
        return {
            slot: remote(
                send, recv.at[slot], stat_ss.at[it, slot], stat_rs.at[it, slot], device
            )
            for slot, _, device in column
        }

    for load in loads:
        load.wait()
    st1[...] = lax.dot_general(
        cs[...], xs[my_rows, :], NT, preferred_element_type=jnp.float32
    ) - 0.5 * norms(cs[...])
    pl.semaphore_wait(barrier, len(column) + 3)
    top, lifted, total = soften(st1[...])
    stat_send1[0:1, :] = top
    stat_send1[1:2, :] = total
    arrivals = send_stats(0, stat_send1, stat_recv1)
    st1[...] = lifted
    lifted_flight = remote(st1.at[other_half], er, e_ss.at[0], e_rs.at[0], (sibling, z))
    x_flights = [
        remote(
            xs.at[my_rows, cols(j)], xs.at[my_rows, cols(j)],
            x_ss.at[j], x_rs.at[j], (sibling, z),
        )
        for j in range(chunks)
    ]

    for it in range(ITERS):
        if it == 0:
            for slot, _, _ in column:
                arrivals[slot].wait_recv()
            stats = [
                (flip, (stat_recv1[slot, 0:1, :], stat_recv1[slot, 1:2, :]))
                for slot, flip, _ in sorted(column, key=lambda entry: entry[0])
            ]
            own = [(top, total)] + [found for flip, found in stats if flip == 0]
            others = [found for flip, found in stats if flip == 1]
            all_top, all_total = combine(own)
            energy_parts = (all_top, all_total)
            scale = jnp.exp(top - all_top) / all_total
            wt[:, my_rows] = (st1[my_half, :] * scale).astype(jnp.bfloat16)
            all_top, all_total = combine(others)
            scale = jnp.exp(others[0][0] - all_top) / all_total
            lifted_flight.wait_recv()
            wt[:, other_rows] = (er[...] * scale).astype(jnp.bfloat16)
        else:
            top, lifted, total = soften(st2[...] - 0.5 * sq[...])
            stat_send2[0:1, :] = top
            stat_send2[1:2, :] = total
            arrivals = send_stats(1, stat_send2, stat_recv2)
            st2[...] = lifted
            for slot, _, _ in column:
                arrivals[slot].wait_recv()
            all_top, all_total = combine(
                [(top, total)]
                + [(stat_recv2[s, 0:1, :], stat_recv2[s, 1:2, :]) for s, _, _ in column]
            )
            scale = jnp.exp(top - all_top) / all_total
            wt[...] = (st2[...] * scale).astype(jnp.bfloat16)

        masses = []
        flights = {}

        def sums(j, it=it):
            if it == 0:
                x_flights[j].wait_recv()
            both = jnp.dot(wt[...], xs[:, cols(j)], preferred_element_type=jnp.float32)
            k0[j] = both
            s1[it, j] = both.astype(jnp.bfloat16)
            for p in (2, 0, 1):
                flights[1 + p, j] = remote(
                    s1.at[it, j, part(chip + flips[p])], r1.at[it, j, p],
                    ring_ss.at[it, j, 1 + p], ring_rs.at[it, j, 1 + p],
                    (r + 2 * flips[p], z),
                )

        def send_masses(it=it):
            mass_send[it] = lax.dot_general(
                jnp.ones((8, 2 * rows), jnp.bfloat16), wt[...], NT,
                preferred_element_type=jnp.float32,
            )[0:1, :]
            for p in range(3):
                masses.append(
                    remote(
                        mass_send.at[it], mass_recv.at[it, p],
                        mass_ss.at[it, p], mass_rs.at[it, p],
                        (r + 2 * flips[p], z),
                    )
                )

        def take_masses(it=it):
            everyone = mass_send[it]
            for p in range(3):
                masses[p].wait_recv()
                everyone = everyone + mass_recv[it, p]
            tall = jnp.broadcast_to(everyone, (128, half))
            mass_col[...] = 1.0 / (jnp.transpose(tall) + PRIOR_WEIGHT)

        def spot(j, rows_of, it=it):
            if it == ITERS - 1:
                return out_ref.at[rows_of, cols(j)]
            return cc.at[it, j, rows_of]

        def share_out(j, n, here, it=it):
            block = spot(j, here)
            flights[7 + n, j] = remote(
                block, block, ring_ss.at[it, j, 7 + n], ring_rs.at[it, j, 7 + n], (sibling, z)
            )

        def update(j, it=it):
            mine = place(core, chip)
            old = cs[mine, cols(j)] if it == 0 else cc[it - 1, j, mine]
            blend = k0[j, part(chip)] + PRIOR_WEIGHT * old.astype(jnp.float32)
            for p in range(3):
                flights[1 + p, j].wait_recv()
                blend = blend + r1[it, j, p].astype(jnp.float32)
            here = spot(j, mine)
            here[...] = (blend * mass_col[part(chip), 0:1]).astype(jnp.bfloat16)
            for p in (2, 0, 1):
                flights[4 + p, j] = remote(
                    here, here, ring_ss.at[it, j, 4 + p], ring_rs.at[it, j, 4 + p],
                    (r + 2 * flips[p], z),
                )
            if it == ITERS - 1:
                share_out(j, 0, mine)

        def gather(j, it=it):
            for p in range(3):
                flights[4 + p, j].wait_recv()
                if it == ITERS - 1:
                    share_out(j, 1 + p, place(core, chip + flips[p]))
            if it < ITERS - 1:
                block = cc[it, j, my_half]
                inner = lax.dot_general(
                    block, xs[:, cols(j)], NT, preferred_element_type=jnp.float32
                )
                if j == 0:
                    st2[...] = inner
                    sq[...] = norms(block)
                else:
                    st2[...] += inner
                    sq[...] += norms(block)

        def finish(j):
            for p in range(4):
                flights[7 + p, j].wait_recv()

        send_masses()
        for j in range(chunks):
            sums(j)
        if it == 0:
            energy_ref[...] = energy_parts[0] + jnp.log(energy_parts[1])
        take_masses()
        for j in range(chunks):
            update(j)
        for j in range(chunks):
            gather(j)
        if it == ITERS - 1:
            for j in range(chunks):
                finish(j)

    for copy in sends:
        copy.wait_send()


def local_fused(groups, embeddings, centroids):
    rows, depth = embeddings.shape
    count = centroids.shape[0]
    chunks = CHUNKS
    width = depth // chunks
    half, share = count // 2, count // 8
    peers = 2 * groups - 1
    bf16, f32 = jnp.bfloat16, jnp.float32
    dma = pltpu.SemaphoreType.DMA
    result, energy = pl.pallas_call(
        functools.partial(kernel, groups, chunks),
        out_shape=(
            pltpu.VMEM((count, depth), bf16),
            pltpu.VMEM((1, rows), f32),
        ),
        in_specs=[pl.BlockSpec(memory_space=pl.ANY)] * 2,
        out_specs=(
            pl.BlockSpec(memory_space=pltpu.VMEM),
            pl.BlockSpec(memory_space=pltpu.VMEM),
        ),
        scratch_shapes=[
            pltpu.VMEM((2 * rows, depth), bf16),
            pltpu.VMEM((count, depth), bf16),
            pltpu.VMEM((half, 2 * rows), bf16),
            pltpu.VMEM((count, rows), f32),
            pltpu.VMEM((half, rows), f32),
            pltpu.VMEM((half, 2 * rows), f32),
            pltpu.VMEM((half, 1), f32),
            pltpu.VMEM((half, 128), f32),
            pltpu.VMEM((2, rows), f32),
            pltpu.VMEM((peers, 2, rows), f32),
            pltpu.VMEM((2, 2 * rows), f32),
            pltpu.VMEM((peers, 2, 2 * rows), f32),
            pltpu.VMEM((ITERS, 1, half), f32),
            pltpu.VMEM((ITERS, 3, 1, half), f32),
            pltpu.VMEM((chunks, half, width), f32),
            pltpu.VMEM((ITERS, chunks, half, width), bf16),
            pltpu.VMEM((ITERS, chunks, 3, share, width), bf16),
            pltpu.VMEM((ITERS - 1, chunks, count, width), bf16),
            dma((2,)),
            dma((chunks,)),
            dma((chunks,)),
            dma((1,)),
            dma((1,)),
            dma((ITERS, peers)),
            dma((ITERS, peers)),
            dma((ITERS, 3)),
            dma((ITERS, 3)),
            dma((ITERS, chunks, 11)),
            dma((ITERS, chunks, 11)),
        ],
        compiler_params=pltpu.CompilerParams(
            collective_id=0, has_side_effects=True, vmem_limit_bytes=63 * 1024 * 1024
        ),
        cost_estimate=pl.CostEstimate(
            flops=8 * rows * count * depth,
            bytes_accessed=2 * depth * (rows + 2 * count),
            transcendentals=2 * rows * count,
        ),
    )(embeddings, centroids)
    return result, energy.reshape(rows)


def solution(mesh):
    def local(embeddings, centroids):
        rows, depth = embeddings.shape
        count = centroids.shape[0]
        groups = mesh.shape["cent"]
        fits = (
            mesh.shape["row"] == 8
            and groups > 1
            and rows % 256 == 0
            and rows <= 1024
            and count == 256
            and depth % (128 * CHUNKS) == 0
        )
        if fits:
            return local_fused(groups, embeddings, centroids)
        return local_plain(embeddings, centroids)

    return jax.shard_map(
        local,
        mesh=mesh,
        in_specs=(P("row", None), P("cent", None)),
        out_specs=(P("cent", None), P("row")),
        check_vma=False,
    )
```
